32 devices in a mesh: blk: 8 (over z, x), rep: 4 (over y, core).
Axes of the slice: x: 2, y: 2, z: 4, core: 2. Of those that a mesh axis runs over, the one named last changes fastest.
Arguments:
- features: bfloat16 [32768, 128], P(('blk', 'rep')), may hold values from -6 to 6
- weight: bfloat16 [128, 512], replicated, may hold values from -0.5 to 0.5
- bias: float32 [512], replicated, may hold values from -3 to 3
- tile_values: bfloat16 [32768, 4096], P(('blk', 'rep')), may hold values from -0.125 to 0.125
- tile_cols: int32 [256, 32], P(('blk', 'rep')), may hold values from 0 to 95, as said below
- tile_counts: int32 [256], P(('blk', 'rep')), may hold values from 1 to 32, as said below
- out_grad: bfloat16 [32768, 512], P(('blk', 'rep')), may hold values from -6 to 6
Outputs:
- activations: bfloat16 [32768, 512], P(('blk', 'rep'))
- feature_grad: float32 [32768, 128], P(('blk', 'rep'))
- weight_grad: float32 [128, 512], replicated
- bias_grad: float32 [512], replicated
The draws below stay inside these ranges and needn't reach their ends.
Inputs may be any that keep to these rules, and one draw needn't show every extreme that they name: `tile_cols`: within one row tile the 32 entries are different. `tile_counts`: slots 0 to count - 1 of a row tile are live.
All inputs are finite; a program needn't handle non-finite values.
Results may differ from the reference program's by a relative error of at most 0.0059.
Values may be sent and summed in bfloat16 or wider, within the bound.
A program may use at most 128 MiB of HBM per device.

```python
import jax
import jax.numpy as jnp
from jax import lax

IN_DIM = 128
OUT_DIM = 512
TILE = 128
REACH = 1
SLOTS = 32
NODES = 32768
BLK_TILES = 32
ROW_TILES = 256
N_BLK = 8


def draw_tile_cols(key, part):
    window_tiles = (2 * REACH + 1) * BLK_TILES
    subkeys = jax.random.split(jax.random.fold_in(key, 11), ROW_TILES)
    chosen = jax.vmap(lambda subkey: jax.random.permutation(subkey, window_tiles)[:SLOTS])(subkeys)
    return chosen.astype(jnp.int32)


def draw_tile_counts(key, part):
    counts = jax.random.randint(jax.random.fold_in(key, 21), (ROW_TILES,), 1, SLOTS + 1)
    fullest = jax.random.randint(jax.random.fold_in(key, 22), (), 0, ROW_TILES)
    return jnp.where(jnp.arange(ROW_TILES) == fullest, SLOTS, counts).astype(jnp.int32)


def levels(own_key, shape, pieces, smallest, largest):
    def one(dim, shards_of):
        heights = jax.random.uniform(jax.random.fold_in(jax.random.fold_in(own_key, 6), dim), (shards_of,), jnp.float32, smallest / len(pieces), largest / len(pieces))
        return jnp.repeat(jnp.exp(heights), shape[dim] // shards_of).reshape((-1,) + (1,) * (len(shape) - dim - 1))

    factor_of = one(*pieces[0])
    for cut in pieces[1:]:
        factor_of = factor_of * one(*cut)
    return factor_of


def scatter_about(own_key, extent, deviation, reach, shards=(), kind=jnp.bfloat16):
    array = deviation * jax.random.normal(own_key, extent, jnp.float32)
    if shards:
        array = array * levels(own_key, extent, shards, -0.22, 0.18)
    return jnp.clip(array, -reach, reach).astype(kind)


def setup_inputs(seed: int = 0) -> dict:
    key_of = jax.random.split(jax.random.key(seed), 8)
    features = scatter_about(key_of[0], (NODES, IN_DIM), 1.0, 6.0, ((0, 32),))
    weight = scatter_about(key_of[1], (IN_DIM, OUT_DIM), IN_DIM ** -0.5, 0.5)
    bias = scatter_about(key_of[2], (OUT_DIM,), 0.5, 3.0, (), jnp.float32)
    tile_values = scatter_about(key_of[3], (NODES, SLOTS * TILE), (SLOTS * TILE // 2) ** -0.5, 0.125, ((0, 32),))
    tile_cols = draw_tile_cols(jax.random.fold_in(key_of[7], 71), 0)
    tile_counts = draw_tile_counts(jax.random.fold_in(key_of[7], 71), 0)
    out_grad = scatter_about(key_of[6], (NODES, OUT_DIM), 1.0, 6.0, ((0, 32),))
    return dict(features=features, weight=weight, bias=bias, tile_values=tile_values, tile_cols=tile_cols, tile_counts=tile_counts, out_grad=out_grad)


def gelu_parts(pre_act):
    inner = 0.7978845608028654 * (pre_act + 0.044715 * pre_act * pre_act * pre_act)
    tangent = jnp.tanh(inner)
    value_part = 0.5 * pre_act * (1.0 + tangent)
    slope = 0.5 * (1.0 + tangent) + 0.5 * pre_act * (1.0 - tangent * tangent) * 0.7978845608028654 * (1.0 + 0.134145 * pre_act * pre_act)
    return value_part, slope


def reference(features, weight, bias, tile_values, tile_cols, tile_counts, out_grad):
    row_ids = jnp.arange(ROW_TILES).astype(jnp.int32)
    row_block = (row_ids // BLK_TILES).astype(jnp.int32)
    block_offset = (tile_cols // BLK_TILES - REACH).astype(jnp.int32)
    col_block = ((row_block[:, None] + block_offset + N_BLK) % N_BLK).astype(jnp.int32)
    global_tile = (col_block * BLK_TILES + tile_cols % BLK_TILES).astype(jnp.int32)
    is_live = jnp.arange(SLOTS).astype(jnp.int32)[None, :] < tile_counts[:, None]
    feature_tiles = features.reshape(ROW_TILES, TILE, IN_DIM)
    value_tiles = tile_values.reshape(ROW_TILES, TILE, SLOTS * TILE)

    def forward_tile(packed):
        tile_block, targets, alive = packed
        gathered = feature_tiles[targets]
        gathered = jnp.where(alive[:, None, None], gathered, jnp.zeros((), gathered.dtype))
        return jnp.dot(tile_block, gathered.reshape(SLOTS * TILE, IN_DIM), preferred_element_type=jnp.float32)

    summed = lax.map(forward_tile, (value_tiles, global_tile, is_live))
    aggregated = summed.reshape(NODES, IN_DIM).astype(jnp.bfloat16)
    pre_act = jnp.dot(aggregated, weight, preferred_element_type=jnp.float32) + bias
    value_part, slope = gelu_parts(pre_act)
    activations = value_part.astype(jnp.bfloat16)
    pre_grad = (out_grad.astype(jnp.float32) * slope).astype(jnp.bfloat16)
    factor = NODES ** -0.5
    weight_grad = jnp.dot(aggregated.T, pre_grad, preferred_element_type=jnp.float32) * factor
    bias_grad = jnp.sum(pre_grad.astype(jnp.float32), axis=0) * factor
    row_grad = jnp.dot(pre_grad, weight.T, preferred_element_type=jnp.float32).astype(jnp.bfloat16)
    grad_tiles = row_grad.reshape(ROW_TILES, TILE, IN_DIM)

    def backward_tile(running, packed):
        tile_block, targets, alive, grad_rows = packed
        partial_value = jnp.dot(tile_block.T, grad_rows, preferred_element_type=jnp.float32).reshape(SLOTS, TILE, IN_DIM)
        partial_value = jnp.where(alive[:, None, None], partial_value, jnp.zeros((), partial_value.dtype))
        return running.at[targets].add(partial_value), None

    initial = jnp.zeros((ROW_TILES, TILE, IN_DIM), jnp.float32)
    feature_grad, unused = lax.scan(backward_tile, initial, (value_tiles, global_tile, is_live, grad_tiles))
    return (activations, feature_grad.reshape(NODES, IN_DIM), weight_grad, bias_grad)
```

```python
import functools
import math

import jax
import jax.numpy as jnp
from jax import lax
from jax.experimental import pallas as pl
from jax.experimental.pallas import tpu as pltpu
from jax.sharding import PartitionSpec as P

TILE = 128
SIDES = 3
GROUP = 4
CHUNKS = 4
SPAN = 8
BIAS_ROWS = 8
MESH = pl.DeviceIdType.MESH
VMEM = pl.BlockSpec(memory_space=pltpu.VMEM)
SMEM = pl.BlockSpec(memory_space=pltpu.SMEM)
ANY = pl.BlockSpec(memory_space=pl.ANY)
LIMIT = 56 * 1024 * 1024


def partners():
    rep = lax.axis_index("rep")
    return rep + 1 - 2 * (rep % 2), (rep + 2) % GROUP


def gather_kernel(count, own_ref, win_ref, own_sem, blk_send, blk_recv, far_send, far_recv,
                  near_send, near_recv):
    blk, rep = lax.axis_index("blk"), lax.axis_index("rep")
    near, far = partners()
    across = (near + 2) % GROUP
    before, after = (blk + count - 1) % count, (blk + 1) % count
    rows = own_ref.shape[0] // CHUNKS

    barrier = pltpu.get_barrier_semaphore()
    for device in ((before, rep), (after, rep), (blk, near), (blk, far)):
        pl.semaphore_signal(barrier, inc=1, device_id=device, device_id_type=MESH)
    pl.semaphore_wait(barrier, 4)

    def part(side, member, chunk):
        return win_ref.at[side, member, pl.ds(chunk * rows, rows)]

    def remote(source, target, send, recv, device):
        return pltpu.make_async_remote_copy(
            src_ref=source, dst_ref=target, send_sem=send, recv_sem=recv,
            device_id=device, device_id_type=MESH)

    def to_blk(which, chunk):
        side, device = ((0, (after, rep)), (2, (before, rep)))[which]
        return remote(own_ref.at[pl.ds(chunk * rows, rows)], part(side, rep, chunk),
                      blk_send.at[which, chunk], blk_recv.at[which, chunk], device)

    def to_far(side, chunk):
        source = own_ref.at[pl.ds(chunk * rows, rows)] if side == 1 else part(side, rep, chunk)
        return remote(source, part(side, rep, chunk), far_send.at[side, chunk],
                      far_recv.at[side, chunk], (blk, far))

    def to_near(side, whose, chunk):
        member = (rep, far)[whose]
        source = part(side, member, chunk)
        if side == 1 and whose == 0:
            source = own_ref.at[pl.ds(chunk * rows, rows)]
        return remote(source, part(side, member, chunk), near_send.at[side, whose, chunk],
                      near_recv.at[side, whose, chunk], (blk, near))

    started = []

    def start(copy):
        copy.start()
        started.append(copy)
        return copy

    local = pltpu.make_async_copy(own_ref, win_ref.at[1, rep], own_sem)
    blk_copies, far_copies, near_copies = {}, {}, {}
    for chunk in range(CHUNKS):
        for which in range(2):
            blk_copies[which, chunk] = start(to_blk(which, chunk))
        far_copies[1, chunk] = start(to_far(1, chunk))
    for chunk in range(CHUNKS):
        near_copies[1, 0, chunk] = start(to_near(1, 0, chunk))
    local.start()
    for chunk in range(CHUNKS):
        for which in range(2):
            blk_copies[which, chunk].wait_recv()
            side = (0, 2)[which]
            far_copies[side, chunk] = start(to_far(side, chunk))
            near_copies[side, 0, chunk] = start(to_near(side, 0, chunk))
    for side in (1, 0, 2):
        for chunk in range(CHUNKS):
            far_copies[side, chunk].wait_recv()
            near_copies[side, 1, chunk] = start(to_near(side, 1, chunk))
    for copy in near_copies.values():
        copy.wait_recv()
    for copy in started:
        copy.wait_send()
    local.wait()


def gather(features):
    rows, width = features.shape
    dma = pltpu.SemaphoreType.DMA
    return pl.pallas_call(
        functools.partial(gather_kernel, lax.axis_size("blk")),
        out_shape=jax.ShapeDtypeStruct((SIDES, GROUP, rows, width), features.dtype),
        in_specs=[VMEM],
        out_specs=VMEM,
        scratch_shapes=[
            dma, dma((2, CHUNKS)), dma((2, CHUNKS)), dma((SIDES, CHUNKS)), dma((SIDES, CHUNKS)),
            dma((SIDES, 2, CHUNKS)), dma((SIDES, 2, CHUNKS)),
        ],
        compiler_params=pltpu.CompilerParams(
            collective_id=0, has_side_effects=True, vmem_limit_bytes=LIMIT),
        name="gather_window",
    )(features)


def gelu_parts(pre_act):
    inner = 0.7978845608028654 * (pre_act + 0.044715 * pre_act * pre_act * pre_act)
    tangent = jnp.tanh(inner)
    half = 0.5 * (1.0 + tangent)
    value_part = pre_act * half
    slope = half + 0.5 * pre_act * (
        1.0 - tangent * tangent
    ) * 0.7978845608028654 * (1.0 + 0.134145 * pre_act * pre_act)
    return value_part, slope


def layer_kernel(factor, counts, cols, win_hbm, val_hbm, weight, bias, og_hbm, act_out, terms_out,
                 grad_out, vals, win, og, placed, agg, pre_grad, row_grad, acc, bias_sum, val_sem,
                 win_sem, og_sem):
    tiles, _, wide = vals.shape
    spans = wide // (SPAN * TILE)
    win_copy = pltpu.make_async_copy(win_hbm, win, win_sem)
    og_copy = pltpu.make_async_copy(og_hbm, og, og_sem)

    def val_copy(t):
        return pltpu.make_async_copy(val_hbm.at[pl.ds(t * TILE, TILE)], vals.at[t], val_sem.at[t])

    win_copy.start()
    for t in range(tiles):
        val_copy(t).start()
    og_copy.start()

    def clear(w, carry):
        placed[w] = jnp.zeros(placed.shape[1:], placed.dtype)
        return carry

    lax.fori_loop(0, placed.shape[0], clear, 0)
    win_copy.wait()

    def forward(t, carry):
        val_copy(t).wait()
        live = counts[t]
        acc[...] = jnp.zeros_like(acc)
        for span in range(spans):

            @pl.when(span * SPAN < live)
            def _():
                picked = []
                for k in range(SPAN):
                    tile = win[cols[t, span * SPAN + k]]
                    picked.append(jnp.where(span * SPAN + k < live, tile, jnp.zeros_like(tile)))
                acc[...] += jnp.dot(
                    vals[t, :, span * SPAN * TILE:(span + 1) * SPAN * TILE],
                    jnp.concatenate(picked, axis=0), preferred_element_type=jnp.float32)

        agg[pl.ds(pl.multiple_of(t * TILE, TILE), TILE)] = acc[...].astype(agg.dtype)
        return carry

    lax.fori_loop(0, tiles, forward, 0)
    og_copy.wait()
    bias_sum[...] = jnp.zeros_like(bias_sum)

    def dense(t, carry):
        here = pl.ds(pl.multiple_of(t * TILE, TILE), TILE)
        pre_act = jnp.dot(agg[here], weight[...], preferred_element_type=jnp.float32) + bias[...]
        value_part, slope = gelu_parts(pre_act)
        act_out[here] = value_part.astype(act_out.dtype)
        grad = (og[here].astype(jnp.float32) * slope).astype(jnp.bfloat16)
        pre_grad[here] = grad
        bias_sum[...] += jnp.sum(
            grad.astype(jnp.float32).reshape(TILE // 8, 8, grad.shape[1]), axis=0)
        row_grad[t] = lax.dot_general(
            weight[...], grad, (((1,), (1,)), ((), ())), preferred_element_type=jnp.float32
        ).astype(row_grad.dtype)
        return carry

    lax.fori_loop(0, tiles, dense, 0)
    weight_grad = lax.dot_general(
        agg[...], pre_grad[...], (((0,), (0,)), ((), ())), preferred_element_type=jnp.float32
    ) * factor
    bias_grad = jnp.sum(bias_sum[...], axis=0, keepdims=True) * factor
    members, blocks = grad_out.shape[:2]
    share = grad_out.shape[2] - BIAS_ROWS
    cut = grad_out.shape[3]
    for member in range(members):
        columns = slice(member * cut, (member + 1) * cut)
        grad_out[member, :, :share, :] = weight_grad[:, columns].reshape(blocks, share, cut)
        grad_out[member, :, share:, :] = jnp.broadcast_to(
            bias_grad[:, columns][None], (blocks, BIAS_ROWS, cut))

    def backward(t, carry):
        live = counts[t]
        for span in range(spans):

            @pl.when(span * SPAN < live)
            def _():
                terms = jnp.dot(
                    row_grad[t], vals[t, :, span * SPAN * TILE:(span + 1) * SPAN * TILE],
                    preferred_element_type=jnp.float32)
                for k in range(SPAN):
                    term = terms[:, k * TILE:(k + 1) * TILE]
                    term = jnp.where(span * SPAN + k < live, term, jnp.zeros_like(term))
                    placed[cols[t, span * SPAN + k]] += term

        return carry

    lax.fori_loop(0, tiles, backward, 0)

    def hand_on(w, carry):
        terms_out[w] = placed[w].astype(terms_out.dtype)
        return carry

    lax.fori_loop(0, placed.shape[0], hand_on, 0)


def layer(counts, cols, window, values, weight, bias, out_grad, factor, blocks):
    rows, wide = values.shape
    in_dim, out_dim = weight.shape
    tiles = rows // TILE
    window_tiles = SIDES * GROUP * tiles
    dma = pltpu.SemaphoreType.DMA
    window_shape = (window_tiles, TILE, in_dim)
    grad_shape = (GROUP, blocks, in_dim // blocks + BIAS_ROWS, out_dim // GROUP)
    return pl.pallas_call(
        functools.partial(layer_kernel, factor),
        out_shape=(
            jax.ShapeDtypeStruct((rows, out_dim), jnp.bfloat16),
            jax.ShapeDtypeStruct((window_tiles, in_dim, TILE), jnp.bfloat16),
            jax.ShapeDtypeStruct(grad_shape, jnp.float32),
        ),
        in_specs=[SMEM, SMEM, ANY, ANY, VMEM, VMEM, ANY],
        out_specs=(VMEM, VMEM, VMEM),
        scratch_shapes=[
            pltpu.VMEM((tiles, TILE, wide), jnp.bfloat16),
            pltpu.VMEM(window_shape, jnp.bfloat16),
            pltpu.VMEM((rows, out_dim), jnp.bfloat16),
            pltpu.VMEM((window_tiles, in_dim, TILE), jnp.float32),
            pltpu.VMEM((rows, in_dim), jnp.bfloat16),
            pltpu.VMEM((rows, out_dim), jnp.bfloat16),
            pltpu.VMEM((tiles, in_dim, TILE), jnp.bfloat16),
            pltpu.VMEM((TILE, in_dim), jnp.float32),
            pltpu.VMEM((8, out_dim), jnp.float32),
            dma((tiles,)), dma, dma,
        ],
        compiler_params=pltpu.CompilerParams(vmem_limit_bytes=LIMIT),
        name="layer",
    )(counts, cols, window.reshape(window_shape), values, weight, bias.reshape(1, -1), out_grad)


def reduce_kernel(count, terms, grads, out_ref, weight_out, bias_out, near_buf, far_out, far_buf,
                  blk_out, blk_buf, rep_buf, share_buf, share_out, whole, near_send, near_recv,
                  far_send, far_recv, blk_send, blk_recv, rep_send, rep_recv, share_send,
                  share_recv, back_send, back_recv, last_send, last_recv):
    blk, rep = lax.axis_index("blk"), lax.axis_index("rep")
    near, far = partners()
    across = (near + 2) % GROUP
    before, after = (blk + count - 1) % count, (blk + 1) % count
    tiles = out_ref.shape[0] // TILE
    step = tiles // CHUNKS
    f32 = jnp.float32

    barrier = pltpu.get_barrier_semaphore()
    for turn in range(1, GROUP):
        pl.semaphore_signal(
            barrier, inc=1, device_id=(blk, (rep + turn) % GROUP), device_id_type=MESH)
    for turn in range(1, count):
        pl.semaphore_signal(
            barrier, inc=1, device_id=((blk + turn) % count, rep), device_id_type=MESH)
    pl.semaphore_wait(barrier, GROUP + count - 2)

    started = []

    def start(source, target, send, recv, device):
        copy = pltpu.make_async_remote_copy(
            src_ref=source, dst_ref=target, send_sem=send, recv_sem=recv,
            device_id=device, device_id_type=MESH)
        copy.start()
        started.append(copy)
        return copy

    near_copies, far_copies, blk_copies = {}, {}, {}
    for whose, side in ((1, 0), (1, 2), (1, 1), (0, 0), (0, 2), (0, 1)):
        near_copies[side, whose] = start(
            terms.at[side, (near, across)[whose]], near_buf.at[side, whose],
            near_send.at[side, whose], near_recv.at[side, whose], (blk, near))
    rep_copies = [
        start(grads.at[(rep + turn) % GROUP], rep_buf.at[turn - 1], rep_send.at[turn - 1],
              rep_recv.at[turn - 1], (blk, (rep + turn) % GROUP))
        for turn in range(1, GROUP)
    ]

    for side in (0, 2, 1):
        near_copies[side, 1].wait_recv()
        for chunk in range(CHUNKS):
            here = pl.ds(chunk * step, step)
            far_out[side, here] = (
                terms[side, far, here].astype(f32) + near_buf[side, 1, here].astype(f32)
            ).astype(far_out.dtype)
            far_copies[side, chunk] = start(
                far_out.at[side, here], far_buf.at[side, here], far_send.at[side, chunk],
                far_recv.at[side, chunk], (blk, far))

    for copy in rep_copies:
        copy.wait_recv()
    share_out[...] = ((grads[rep] + rep_buf[0]) + rep_buf[1]) + rep_buf[2]
    share_copies = [
        start(share_out.at[(blk + turn) % count], share_buf.at[turn - 1], share_send.at[turn - 1],
              share_recv.at[turn - 1], ((blk + turn) % count, rep))
        for turn in range(1, count)
    ]

    for side in (0, 2, 1):
        near_copies[side, 0].wait_recv()
    for chunk in range(CHUNKS):
        here = pl.ds(chunk * step, step)
        for which, side in ((0, 0), (1, 2)):
            far_copies[side, chunk].wait_recv()
            blk_out[which, here] = (
                terms[side, rep, here].astype(f32) + near_buf[side, 0, here].astype(f32)
                + far_buf[side, here].astype(f32)
            ).astype(blk_out.dtype)
            blk_copies[which, chunk] = start(
                blk_out.at[which, here], blk_buf.at[which, here], blk_send.at[which, chunk],
                blk_recv.at[which, chunk], ((before, after)[which], rep))
        if chunk == CHUNKS // 2 - 1:
            for copy in share_copies:
                copy.wait_recv()
            total = share_out[blk]
            for turn in range(1, count):
                total += share_buf[turn - 1]
            whole[rep, blk] = total
            back_copies = [
                start(whole.at[rep, blk], whole.at[rep, blk], back_send.at[turn - 1],
                      back_recv.at[turn - 1], ((blk + turn) % count, rep))
                for turn in range(1, count)
            ]

    for copy in back_copies:
        copy.wait_recv()
    last_copies = [
        start(whole.at[rep], whole.at[rep], last_send.at[turn - 1], last_recv.at[turn - 1],
              (blk, (rep + turn) % GROUP))
        for turn in range(1, GROUP)
    ]

    for chunk in range(CHUNKS):
        far_copies[1, chunk].wait_recv()
        here = pl.ds(chunk * step, step)
        total = (
            terms[1, rep, here].astype(f32) + near_buf[1, 0, here].astype(f32)
            + far_buf[1, here].astype(f32)
        )
        for which in range(2):
            blk_copies[which, chunk].wait_recv()
            total += blk_buf[which, here].astype(f32)
        for k in range(step):
            out_ref[pl.ds((chunk * step + k) * TILE, TILE)] = total[k].T

    for copy in last_copies:
        copy.wait_recv()
    blocks, share = whole.shape[1], whole.shape[2] - BIAS_ROWS
    cut = whole.shape[3]
    for member in range(GROUP):
        columns = slice(member * cut, (member + 1) * cut)
        weight_out[:, columns] = whole[member, :, :share, :].reshape(blocks * share, cut)
        bias_out[:, columns] = whole[member, 0, share:share + 1, :]
    for copy in started:
        copy.wait_send()


def reduce(terms, grads, rows):
    count = lax.axis_size("blk")
    tiles, in_dim, _ = terms.shape
    tiles = tiles // (SIDES * GROUP)
    terms = terms.reshape(SIDES, GROUP, tiles, in_dim, TILE)
    _, blocks, share, cut = grads.shape
    piece = (tiles, in_dim, TILE)
    dma = pltpu.SemaphoreType.DMA
    pairs = [(SIDES, 2), (SIDES, CHUNKS), (2, CHUNKS), (GROUP - 1,), (count - 1,), (count - 1,),
             (GROUP - 1,)]
    return pl.pallas_call(
        functools.partial(reduce_kernel, count),
        out_shape=(
            jax.ShapeDtypeStruct((rows, in_dim), jnp.float32),
            jax.ShapeDtypeStruct((in_dim, GROUP * cut), jnp.float32),
            jax.ShapeDtypeStruct((1, GROUP * cut), jnp.float32),
        ),
        in_specs=[VMEM, VMEM],
        out_specs=(VMEM, VMEM, VMEM),
        scratch_shapes=[
            pltpu.VMEM((SIDES, 2) + piece, jnp.bfloat16),
            pltpu.VMEM((SIDES,) + piece, jnp.bfloat16),
            pltpu.VMEM((SIDES,) + piece, jnp.bfloat16),
            pltpu.VMEM((2,) + piece, jnp.bfloat16),
            pltpu.VMEM((2,) + piece, jnp.bfloat16),
            pltpu.VMEM((GROUP - 1, blocks, share, cut), jnp.float32),
            pltpu.VMEM((blocks - 1, share, cut), jnp.float32),
            pltpu.VMEM((blocks, share, cut), jnp.float32),
            pltpu.VMEM((GROUP, blocks, share, cut), jnp.float32),
        ] + [dma(shape) for shape in pairs for _ in range(2)],
        compiler_params=pltpu.CompilerParams(
            collective_id=1, has_side_effects=True, vmem_limit_bytes=LIMIT),
        name="reduce_terms",
    )(terms, grads)


def on_device(features, weight, bias, tile_values, tile_cols, tile_counts, out_grad):
    rows = features.shape[0]
    blocks = lax.axis_size("blk")
    nodes = rows * lax.axis_size("rep") * blocks
    window = gather(features)
    activations, terms, grads = layer(
        tile_counts, tile_cols, window, tile_values, weight, bias, out_grad,
        1.0 / math.sqrt(nodes), blocks)
    feature_grad, weight_grad, bias_grad = reduce(terms, grads, rows)
    return activations, feature_grad, weight_grad, bias_grad.reshape(-1)


def solution(mesh):
    assert mesh.shape["rep"] == GROUP
    rows = P(("blk", "rep"), None)
    return jax.shard_map(
        on_device, mesh=mesh,
        in_specs=(rows, P(), P(), rows, rows, P(("blk", "rep")), rows),
        out_specs=(rows, rows, P(), P()), check_vma=False,
    )
```

```python
import functools
import math

import jax
import jax.numpy as jnp
from jax import lax
from jax.experimental import pallas as pl
from jax.experimental.pallas import tpu as pltpu
from jax.sharding import PartitionSpec as P

TILE = 128
SIDES = 3
GROUP = 4
CHUNKS = 4
SPAN = 8
BIAS_ROWS = 16
SUM_ROWS = 8
MESH = pl.DeviceIdType.MESH
VMEM = pl.BlockSpec(memory_space=pltpu.VMEM)
SMEM = pl.BlockSpec(memory_space=pltpu.SMEM)
ANY = pl.BlockSpec(memory_space=pl.ANY)
LIMIT = 56 * 1024 * 1024


def partners():
    rep = lax.axis_index("rep")
    return rep + 1 - 2 * (rep % 2), (rep + 2) % GROUP


def gather_kernel(count, own_ref, win_ref, own_sem, blk_send, blk_recv, far_send, far_recv,
                  near_send, near_recv, turn_send, turn_recv):
    blk, rep = lax.axis_index("blk"), lax.axis_index("rep")
    near, far = partners()
    before, after = (blk + count - 1) % count, (blk + 1) % count
    rows = own_ref.shape[0] // CHUNKS
    turned = CHUNKS - 1
    plain = range(CHUNKS - 1)

    barrier = pltpu.get_barrier_semaphore()
    for device in ((before, rep), (after, rep), (blk, near), (blk, far)):
        pl.semaphore_signal(barrier, inc=1, device_id=device, device_id_type=MESH)
    pl.semaphore_wait(barrier, 4)

    started = []

    def start(side, member, chunk, send, recv, device, own=False, lands=None):
        here = pl.ds(chunk * rows, rows)
        source = own_ref.at[here] if own else win_ref.at[side, member, here]
        target = win_ref.at[side if lands is None else lands, member, here]
        copy = pltpu.make_async_remote_copy(
            src_ref=source, dst_ref=target, send_sem=send, recv_sem=recv,
            device_id=device, device_id_type=MESH)
        copy.start()
        started.append(copy)
        return copy

    ways = ((0, after), (2, before))

    def to_blk(which, chunk):
        lands, target = ways[which]
        return start(1, rep, chunk, blk_send.at[which, chunk], blk_recv.at[which, chunk],
                     (target, rep), own=True, lands=lands)

    def to_turn(which):
        lands, target = ways[which]
        return start(1, far, turned, turn_send.at[which], turn_recv.at[which], (target, rep),
                     lands=lands)

    def to_far(side, chunk):
        return start(side, rep, chunk, far_send.at[side, chunk], far_recv.at[side, chunk],
                     (blk, far), own=side == 1)

    near_copies = []

    def to_near(side, whose, chunk):
        near_copies.append(start(
            side, (rep, far)[whose], chunk, near_send.at[side, whose, chunk],
            near_recv.at[side, whose, chunk], (blk, near), own=side == 1 and whose == 0))

    blk_copies, far_copies = {}, {}
    far_copies[1, turned] = to_far(1, turned)
    for chunk in range(CHUNKS):
        for which in range(2):
            blk_copies[which, chunk] = to_blk(which, chunk)
        if chunk in plain:
            far_copies[1, chunk] = to_far(1, chunk)
    for chunk in range(CHUNKS):
        to_near(1, 0, chunk)
    local = pltpu.make_async_copy(own_ref, win_ref.at[1, rep], own_sem)
    local.start()

    far_copies[1, turned].wait_recv()
    turns = [to_turn(which) for which in range(2)]
    to_near(1, 1, turned)
    for chunk in range(CHUNKS):
        for which in range(2):
            side = ways[which][0]
            blk_copies[which, chunk].wait_recv()
            if chunk in plain:
                far_copies[side, chunk] = to_far(side, chunk)
            to_near(side, 0, chunk)
    for chunk in plain:
        far_copies[1, chunk].wait_recv()
        to_near(1, 1, chunk)
    for which in range(2):
        turns[which].wait_recv()
        to_near(ways[which][0], 1, turned)
    for chunk in plain:
        for side in (0, 2):
            far_copies[side, chunk].wait_recv()
            to_near(side, 1, chunk)
    for copy in near_copies:
        copy.wait_recv()
    for copy in started:
        copy.wait_send()
    local.wait()


def gather(features):
    rows, width = features.shape
    dma = pltpu.SemaphoreType.DMA
    return pl.pallas_call(
        functools.partial(gather_kernel, lax.axis_size("blk")),
        out_shape=jax.ShapeDtypeStruct((SIDES, GROUP, rows, width), features.dtype),
        in_specs=[VMEM],
        out_specs=VMEM,
        scratch_shapes=[
            dma, dma((2, CHUNKS)), dma((2, CHUNKS)), dma((SIDES, CHUNKS)), dma((SIDES, CHUNKS)),
            dma((SIDES, 2, CHUNKS)), dma((SIDES, 2, CHUNKS)), dma((2,)), dma((2,)),
        ],
        compiler_params=pltpu.CompilerParams(
            collective_id=0, has_side_effects=True, vmem_limit_bytes=LIMIT),
        name="gather_window",
    )(features)


def gelu_parts(pre_act):
    inner = 0.7978845608028654 * (pre_act + 0.044715 * pre_act * pre_act * pre_act)
    tangent = jnp.tanh(inner)
    half = 0.5 * (1.0 + tangent)
    value_part = pre_act * half
    slope = half + 0.5 * pre_act * (
        1.0 - tangent * tangent
    ) * 0.7978845608028654 * (1.0 + 0.134145 * pre_act * pre_act)
    return value_part, slope


def layer_kernel(factor, counts, cols, win_hbm, val_hbm, weight, bias, og_hbm, act_out, terms_out,
                 grad_out, vals, win, og, placed, agg, pre_grad, row_grad, acc, bias_sum, val_sem,
                 win_sem, og_sem):
    tiles, _, wide = vals.shape
    spans = wide // (SPAN * TILE)
    win_copy = pltpu.make_async_copy(win_hbm, win, win_sem)
    og_copy = pltpu.make_async_copy(og_hbm, og, og_sem)

    def val_copy(t):
        return pltpu.make_async_copy(val_hbm.at[pl.ds(t * TILE, TILE)], vals.at[t], val_sem.at[t])

    win_copy.start()
    for t in range(tiles):
        val_copy(t).start()
    og_copy.start()

    def clear(w, carry):
        placed[w] = jnp.zeros(placed.shape[1:], placed.dtype)
        return carry

    lax.fori_loop(0, placed.shape[0], clear, 0)
    win_copy.wait()

    def forward(t, carry):
        val_copy(t).wait()
        live = counts[t]
        acc[...] = jnp.zeros_like(acc)
        for span in range(spans):

            @pl.when(span * SPAN < live)
            def _():
                picked = []
                for k in range(SPAN):
                    tile = win[cols[t, span * SPAN + k]]
                    picked.append(jnp.where(span * SPAN + k < live, tile, jnp.zeros_like(tile)))
                acc[...] += jnp.dot(
                    vals[t, :, span * SPAN * TILE:(span + 1) * SPAN * TILE],
                    jnp.concatenate(picked, axis=0), preferred_element_type=jnp.float32)

        agg[pl.ds(pl.multiple_of(t * TILE, TILE), TILE)] = acc[...].astype(agg.dtype)
        return carry

    lax.fori_loop(0, tiles, forward, 0)
    og_copy.wait()
    bias_sum[...] = jnp.zeros_like(bias_sum)

    def dense(t, carry):
        here = pl.ds(pl.multiple_of(t * TILE, TILE), TILE)
        pre_act = jnp.dot(agg[here], weight[...], preferred_element_type=jnp.float32) + bias[...]
        value_part, slope = gelu_parts(pre_act)
        act_out[here] = value_part.astype(act_out.dtype)
        grad = (og[here].astype(jnp.float32) * slope).astype(jnp.bfloat16)
        pre_grad[here] = grad
        bias_sum[...] += jnp.sum(
            grad.astype(jnp.float32).reshape(TILE // 8, 8, grad.shape[1]), axis=0)
        row_grad[t] = lax.dot_general(
            weight[...], grad, (((1,), (1,)), ((), ())), preferred_element_type=jnp.float32
        ).astype(row_grad.dtype)
        return carry

    lax.fori_loop(0, tiles, dense, 0)
    weight_grad = lax.dot_general(
        agg[...], pre_grad[...], (((0,), (0,)), ((), ())), preferred_element_type=jnp.float32
    ) * factor
    bias_grad = jnp.sum(bias_sum[...], axis=0, keepdims=True) * factor
    members, _, cut = grad_out.shape
    in_dim = agg.shape[1]
    for member in range(members):
        columns = slice(member * cut, (member + 1) * cut)
        grad_out[member, :in_dim] = weight_grad[:, columns].astype(grad_out.dtype)
        grad_out[member, in_dim:] = jnp.broadcast_to(
            bias_grad[:, columns], (BIAS_ROWS, cut)).astype(grad_out.dtype)

    def backward(t, carry):
        live = counts[t]
        for span in range(spans):

            @pl.when(span * SPAN < live)
            def _():
                terms = jnp.dot(
                    row_grad[t], vals[t, :, span * SPAN * TILE:(span + 1) * SPAN * TILE],
                    preferred_element_type=jnp.float32)
                for k in range(SPAN):
                    term = terms[:, k * TILE:(k + 1) * TILE]
                    term = jnp.where(span * SPAN + k < live, term, jnp.zeros_like(term))
                    placed[cols[t, span * SPAN + k]] += term

        return carry

    lax.fori_loop(0, tiles, backward, 0)

    def hand_on(w, carry):
        terms_out[w] = placed[w].astype(terms_out.dtype)
        return carry

    lax.fori_loop(0, placed.shape[0], hand_on, 0)


def layer(counts, cols, window, values, weight, bias, out_grad, factor):
    rows, wide = values.shape
    in_dim, out_dim = weight.shape
    tiles = rows // TILE
    window_tiles = SIDES * GROUP * tiles
    dma = pltpu.SemaphoreType.DMA
    window_shape = (window_tiles, TILE, in_dim)
    grad_shape = (GROUP, in_dim + BIAS_ROWS, out_dim // GROUP)
    return pl.pallas_call(
        functools.partial(layer_kernel, factor),
        out_shape=(
            jax.ShapeDtypeStruct((rows, out_dim), jnp.bfloat16),
            jax.ShapeDtypeStruct((window_tiles, in_dim, TILE), jnp.bfloat16),
            jax.ShapeDtypeStruct(grad_shape, jnp.bfloat16),
        ),
        in_specs=[SMEM, SMEM, ANY, ANY, VMEM, VMEM, ANY],
        out_specs=(VMEM, VMEM, VMEM),
        scratch_shapes=[
            pltpu.VMEM((tiles, TILE, wide), jnp.bfloat16),
            pltpu.VMEM(window_shape, jnp.bfloat16),
            pltpu.VMEM((rows, out_dim), jnp.bfloat16),
            pltpu.VMEM((window_tiles, in_dim, TILE), jnp.float32),
            pltpu.VMEM((rows, in_dim), jnp.bfloat16),
            pltpu.VMEM((rows, out_dim), jnp.bfloat16),
            pltpu.VMEM((tiles, in_dim, TILE), jnp.bfloat16),
            pltpu.VMEM((TILE, in_dim), jnp.float32),
            pltpu.VMEM((8, out_dim), jnp.float32),
            dma((tiles,)), dma, dma,
        ],
        compiler_params=pltpu.CompilerParams(vmem_limit_bytes=LIMIT),
        name="layer",
    )(counts, cols, window.reshape(window_shape), values, weight, bias.reshape(1, -1), out_grad)


def reduce_kernel(count, terms, grads, out_ref, whole, near_buf, far_out, far_buf, blk_out,
                  blk_buf, turn_buf, rep_buf, share_out, share_buf, summed, near_send, near_recv,
                  far_send, far_recv, blk_send, blk_recv, turn_send, turn_recv, rep_send, rep_recv,
                  share_send, share_recv, back_send, back_recv, last_send, last_recv):
    blk, rep = lax.axis_index("blk"), lax.axis_index("rep")
    near, far = partners()
    across = (near + 2) % GROUP
    before, after = (blk + count - 1) % count, (blk + 1) % count
    step = out_ref.shape[0] // CHUNKS
    turned = CHUNKS - 1
    plain = range(CHUNKS - 1)
    f32 = jnp.float32

    barrier = pltpu.get_barrier_semaphore()
    for turn in range(1, GROUP):
        pl.semaphore_signal(
            barrier, inc=1, device_id=(blk, (rep + turn) % GROUP), device_id_type=MESH)
    for turn in range(1, count):
        pl.semaphore_signal(
            barrier, inc=1, device_id=((blk + turn) % count, rep), device_id_type=MESH)
    pl.semaphore_wait(barrier, GROUP + count - 2)

    started = []

    def start(source, target, send, recv, device):
        copy = pltpu.make_async_remote_copy(
            src_ref=source, dst_ref=target, send_sem=send, recv_sem=recv,
            device_id=device, device_id_type=MESH)
        copy.start()
        started.append(copy)
        return copy

    def to_reps(source, target, send, recv):
        return [
            start(source(turn), target(turn), send.at[turn - 1], recv.at[turn - 1],
                  (blk, (rep + turn) % GROUP))
            for turn in range(1, GROUP)
        ]

    def to_blks(source, target, send, recv):
        return [
            start(source(turn), target(turn), send.at[turn - 1], recv.at[turn - 1],
                  ((blk + turn) % count, rep))
            for turn in range(1, count)
        ]

    near_copies, far_copies, blk_copies, turn_copies = {}, {}, {}, {}
    ways = ((0, before), (2, after))

    def to_near(side, whose):
        near_copies[side, whose] = start(
            terms.at[side, (near, across)[whose]], near_buf.at[side, whose],
            near_send.at[side, whose], near_recv.at[side, whose], (blk, near))

    to_near(0, 1)
    to_near(2, 1)
    rep_copies = to_reps(
        lambda turn: grads.at[(rep + turn) % GROUP], lambda turn: rep_buf.at[turn - 1],
        rep_send, rep_recv)
    for side, whose in ((0, 0), (2, 0), (1, 1), (1, 0)):
        to_near(side, whose)

    def here(chunk):
        return pl.ds(chunk * step, step)

    def chip_sum(side, whose, chunk):
        part = here(chunk)
        return (terms[side, (rep, far)[whose], part].astype(f32)
                + near_buf[side, whose, part].astype(f32))

    def to_far(side, chunk, value):
        part = here(chunk)
        far_out[side, part] = value.astype(far_out.dtype)
        far_copies[side, chunk] = start(
            far_out.at[side, part], far_buf.at[side, part], far_send.at[side, chunk],
            far_recv.at[side, chunk], (blk, far))

    def to_blk(which, chunk, value):
        part = here(chunk)
        blk_out[which, part] = value.astype(blk_out.dtype)
        blk_copies[which, chunk] = start(
            blk_out.at[which, part], blk_buf.at[which, part], blk_send.at[which, chunk],
            blk_recv.at[which, chunk], (ways[which][1], rep))

    near_copies[0, 1].wait_recv()
    near_copies[2, 1].wait_recv()
    for which, (side, block) in enumerate(ways):
        part = here(turned)
        far_out[side, part] = chip_sum(side, 1, turned).astype(far_out.dtype)
        turn_copies[which] = start(
            far_out.at[side, part], turn_buf.at[which], turn_send.at[which], turn_recv.at[which],
            (block, rep))
    for chunk in plain:
        for side in (0, 2):
            to_far(side, chunk, chip_sum(side, 1, chunk))

    for copy in rep_copies:
        copy.wait_recv()
    in_dim = grads.shape[1] - BIAS_ROWS
    share = in_dim // count
    total = grads[rep].astype(f32)
    for turn in range(1, GROUP):
        total += rep_buf[turn - 1].astype(f32)
    share_out[:, :share] = total[:in_dim].reshape(count, share, total.shape[1])
    share_out[:, share:] = jnp.broadcast_to(
        total[in_dim:in_dim + SUM_ROWS][None], (count, SUM_ROWS, total.shape[1]))
    share_copies = to_blks(
        lambda turn: share_out.at[(blk + turn) % count], lambda turn: share_buf.at[turn - 1],
        share_send, share_recv)

    near_copies[0, 0].wait_recv()
    near_copies[2, 0].wait_recv()
    for which, (side, _) in enumerate(ways):
        to_blk(which, turned, chip_sum(side, 0, turned))
    near_copies[1, 1].wait_recv()
    for chunk in plain:
        to_far(1, chunk, chip_sum(1, 1, chunk))
    own = chip_sum(1, 1, turned)
    for which in range(2):
        turn_copies[which].wait_recv()
        own += turn_buf[which].astype(f32)
    to_far(1, turned, own)

    for chunk in plain:
        for which, (side, _) in enumerate(ways):
            far_copies[side, chunk].wait_recv()
            to_blk(which, chunk,
                   chip_sum(side, 0, chunk) + far_buf[side, here(chunk)].astype(f32))
        if chunk == 0:
            for copy in share_copies:
                copy.wait_recv()
            mine = share_out[blk]
            for turn in range(1, count):
                mine += share_buf[turn - 1]
            summed[blk] = mine
            back_copies = to_blks(
                lambda turn: summed.at[blk], lambda turn: summed.at[blk], back_send, back_recv)

    for copy in back_copies:
        copy.wait_recv()
    whole[rep, :in_dim] = summed[:, :share].reshape(in_dim, total.shape[1]).astype(whole.dtype)
    whole[rep, in_dim:] = jnp.broadcast_to(
        summed[0, share:share + 1], (BIAS_ROWS, total.shape[1])).astype(whole.dtype)
    last_copies = to_reps(
        lambda turn: whole.at[rep], lambda turn: whole.at[rep], last_send, last_recv)

    near_copies[1, 0].wait_recv()
    for chunk in (turned, *plain):
        part = here(chunk)
        for which in range(2):
            blk_copies[which, chunk].wait_recv()
        far_copies[1, chunk].wait_recv()
        total = chip_sum(1, 0, chunk) + far_buf[1, part].astype(f32)
        for which in range(2):
            total += blk_buf[which, part].astype(f32)
        out_ref[part] = total

    for copy in last_copies:
        copy.wait_recv()
    for copy in started:
        copy.wait_send()


def reduce(terms, grads):
    count = lax.axis_size("blk")
    tiles, in_dim, _ = terms.shape
    tiles = tiles // (SIDES * GROUP)
    terms = terms.reshape(SIDES, GROUP, tiles, in_dim, TILE)
    cut = grads.shape[2]
    share = in_dim // count + SUM_ROWS
    piece = (tiles, in_dim, TILE)
    dma = pltpu.SemaphoreType.DMA
    pairs = [(SIDES, 2), (SIDES, CHUNKS), (2, CHUNKS), (2,), (GROUP - 1,), (count - 1,),
             (count - 1,), (GROUP - 1,)]
    return pl.pallas_call(
        functools.partial(reduce_kernel, count),
        out_shape=(
            jax.ShapeDtypeStruct(piece, jnp.float32),
            jax.ShapeDtypeStruct(grads.shape, jnp.bfloat16),
        ),
        in_specs=[VMEM, VMEM],
        out_specs=(VMEM, VMEM),
        scratch_shapes=[
            pltpu.VMEM((SIDES, 2) + piece, jnp.bfloat16),
            pltpu.VMEM((SIDES,) + piece, jnp.bfloat16),
            pltpu.VMEM((SIDES,) + piece, jnp.bfloat16),
            pltpu.VMEM((2,) + piece, jnp.bfloat16),
            pltpu.VMEM((2,) + piece, jnp.bfloat16),
            pltpu.VMEM((2, tiles // CHUNKS) + piece[1:], jnp.bfloat16),
            pltpu.VMEM((GROUP - 1,) + grads.shape[1:], jnp.bfloat16),
            pltpu.VMEM((count, share, cut), jnp.float32),
            pltpu.VMEM((count - 1, share, cut), jnp.float32),
            pltpu.VMEM((count, share, cut), jnp.float32),
        ] + [dma(shape) for shape in pairs for _ in range(2)],
        compiler_params=pltpu.CompilerParams(
            collective_id=1, has_side_effects=True, vmem_limit_bytes=LIMIT),
        name="reduce_terms",
    )(terms, grads)


def finish_kernel(turned, whole, feature_out, weight_out, bias_out):
    in_dim, cut = weight_out.shape[0], whole.shape[2]
    for tile in range(turned.shape[0]):
        feature_out[tile * TILE:(tile + 1) * TILE] = turned[tile].T
    for member in range(GROUP):
        columns = slice(member * cut, (member + 1) * cut)
        weight_out[:, columns] = whole[member, :in_dim].astype(jnp.float32)
        bias_out[:, columns] = whole[member, in_dim:].astype(jnp.float32)[:1]


def finish(turned, whole):
    tiles, in_dim, _ = turned.shape
    out_dim = GROUP * whole.shape[2]
    return pl.pallas_call(
        finish_kernel,
        out_shape=(
            jax.ShapeDtypeStruct((tiles * TILE, in_dim), jnp.float32),
            jax.ShapeDtypeStruct((in_dim, out_dim), jnp.float32),
            jax.ShapeDtypeStruct((1, out_dim), jnp.float32),
        ),
        in_specs=[VMEM, VMEM],
        out_specs=(VMEM, VMEM, VMEM),
        compiler_params=pltpu.CompilerParams(vmem_limit_bytes=LIMIT),
        name="finish",
    )(turned, whole)


def on_device(features, weight, bias, tile_values, tile_cols, tile_counts, out_grad):
    nodes = features.shape[0] * lax.axis_size("rep") * lax.axis_size("blk")
    window = gather(features)
    activations, terms, grads = layer(
        tile_counts, tile_cols, window, tile_values, weight, bias, out_grad,
        1.0 / math.sqrt(nodes))
    feature_grad, weight_grad, bias_grad = finish(*reduce(terms, grads))
    return activations, feature_grad, weight_grad, bias_grad.reshape(-1)


def solution(mesh):
    assert mesh.shape["rep"] == GROUP
    rows = P(("blk", "rep"), None)
    return jax.shard_map(
        on_device, mesh=mesh,
        in_specs=(rows, P(), P(), rows, rows, P(("blk", "rep")), rows),
        out_specs=(rows, rows, P(), P()), check_vma=False,
    )
```

```python
import functools
import math

import jax
import jax.numpy as jnp
from jax import lax
from jax.experimental import pallas as pl
from jax.experimental.pallas import tpu as pltpu
from jax.sharding import PartitionSpec as P

TILE = 128
SIDES = 3
GROUP = 4
CHUNKS = 4
PLAIN = (0, 1)
TURNED = (2, 3)
SPAN = 8
BIAS_ROWS = 16
SUM_ROWS = 8
MESH = pl.DeviceIdType.MESH
VMEM = pl.BlockSpec(memory_space=pltpu.VMEM)
SMEM = pl.BlockSpec(memory_space=pltpu.SMEM)
ANY = pl.BlockSpec(memory_space=pl.ANY)
LIMIT = 56 * 1024 * 1024


def partners():
    rep = lax.axis_index("rep")
    return rep + 1 - 2 * (rep % 2), (rep + 2) % GROUP


def lines(count):
    blk = lax.axis_index("blk")
    odd = blk % 2
    pair = blk + 1 - 2 * odd
    onward = (blk + 2 - 4 * odd + count) % count
    behind = (blk + 4 * odd - 2 + count) % count
    return pair, onward, behind, 2 * odd, 2 - 2 * odd


def gather_kernel(count, own_ref, win_ref, own_sem, pair_send, pair_recv, on_send, on_recv,
                  far_send, far_recv, near_send, near_recv):
    blk, rep = lax.axis_index("blk"), lax.axis_index("rep")
    near, far = partners()
    pair, onward, behind, on_side, pair_side = lines(count)
    sides = (on_side, 1, pair_side)
    rows = own_ref.shape[0] // CHUNKS

    barrier = pltpu.get_barrier_semaphore()
    for device in ((pair, rep), (onward, rep), (behind, rep), (blk, near), (blk, far)):
        pl.semaphore_signal(barrier, inc=1, device_id=device, device_id_type=MESH)
    pl.semaphore_wait(barrier, 5)

    started = []

    def start(side, member, chunk, lands, send, recv, device):
        here = pl.ds(chunk * rows, rows)
        source = win_ref.at[sides[side], (rep, far)[member], here]
        if side == 1 and member == 0:
            source = own_ref.at[here]
        copy = pltpu.make_async_remote_copy(
            src_ref=source, dst_ref=win_ref.at[sides[lands], (rep, far)[member], here],
            send_sem=send, recv_sem=recv, device_id=device, device_id_type=MESH)
        copy.start()
        started.append(copy)
        return copy

    pair_copies, on_copies, far_copies, near_copies = {}, {}, {}, []

    def to_pair(member, chunk):
        pair_copies[member, chunk] = start(
            1, member, chunk, 0, pair_send.at[member, chunk], pair_recv.at[member, chunk],
            (pair, rep))

    def to_onward(member, chunk):
        on_copies[member, chunk] = start(
            2, member, chunk, 0, on_send.at[member, chunk], on_recv.at[member, chunk],
            (onward, rep))

    def to_far(side, chunk):
        far_copies[side, chunk] = start(
            side, 0, chunk, side, far_send.at[side, chunk], far_recv.at[side, chunk], (blk, far))

    def to_near(side, member, chunk):
        near_copies.append(start(
            side, member, chunk, side, near_send.at[side, member, chunk],
            near_recv.at[side, member, chunk], (blk, near)))

    order = PLAIN + TURNED
    for own, over in zip(order, TURNED + PLAIN):
        to_pair(0, own)
        to_far(1, over)
    for chunk in order:
        to_near(1, 0, chunk)
    local = pltpu.make_async_copy(own_ref, win_ref.at[1, rep], own_sem)
    local.start()

    def pair_came(member, chunk):
        pair_copies[member, chunk].wait_recv()
        to_onward(member, chunk)
        if member == 0 and chunk in PLAIN:
            to_far(2, chunk)
        to_near(2, member, chunk)

    def on_came(member, chunk):
        on_copies[member, chunk].wait_recv()
        if member == 0 and chunk in PLAIN:
            to_far(0, chunk)
        to_near(0, member, chunk)

    def far_came(side, chunk):
        far_copies[side, chunk].wait_recv()
        if side == 1 and chunk in TURNED:
            to_pair(1, chunk)
        to_near(side, 1, chunk)

    for own, over in zip(PLAIN, TURNED):
        far_came(1, over)
        pair_came(0, own)
    for chunk in PLAIN:
        on_came(0, chunk)
    for chunk in TURNED:
        pair_came(0, chunk)
    for chunk in PLAIN:
        far_came(1, chunk)
    for chunk in TURNED:
        pair_came(1, chunk)
        on_came(0, chunk)
    for chunk in PLAIN:
        far_came(2, chunk)
        far_came(0, chunk)
    for chunk in TURNED:
        on_came(1, chunk)
    for copy in near_copies:
        copy.wait_recv()
    for copy in started:
        copy.wait_send()
    local.wait()


def gather(features):
    rows, width = features.shape
    dma = pltpu.SemaphoreType.DMA
    return pl.pallas_call(
        functools.partial(gather_kernel, lax.axis_size("blk")),
        out_shape=jax.ShapeDtypeStruct((SIDES, GROUP, rows, width), features.dtype),
        in_specs=[VMEM],
        out_specs=VMEM,
        scratch_shapes=[
            dma, dma((2, CHUNKS)), dma((2, CHUNKS)), dma((2, CHUNKS)), dma((2, CHUNKS)),
            dma((SIDES, CHUNKS)), dma((SIDES, CHUNKS)), dma((SIDES, 2, CHUNKS)),
            dma((SIDES, 2, CHUNKS)),
        ],
        compiler_params=pltpu.CompilerParams(
            collective_id=0, has_side_effects=True, vmem_limit_bytes=LIMIT),
        name="gather_window",
    )(features)


def gelu_parts(pre_act):
    inner = 0.7978845608028654 * (pre_act + 0.044715 * pre_act * pre_act * pre_act)
    tangent = jnp.tanh(inner)
    half = 0.5 * (1.0 + tangent)
    value_part = pre_act * half
    slope = half + 0.5 * pre_act * (
        1.0 - tangent * tangent
    ) * 0.7978845608028654 * (1.0 + 0.134145 * pre_act * pre_act)
    return value_part, slope


def layer_kernel(factor, counts, cols, win_hbm, val_hbm, weight, bias, og_hbm, act_out, terms_out,
                 grad_out, vals, win, og, placed, agg, pre_grad, row_grad, acc, bias_sum, val_sem,
                 win_sem, og_sem):
    tiles, _, wide = vals.shape
    spans = wide // (SPAN * TILE)
    win_copy = pltpu.make_async_copy(win_hbm, win, win_sem)
    og_copy = pltpu.make_async_copy(og_hbm, og, og_sem)

    def val_copy(t):
        return pltpu.make_async_copy(val_hbm.at[pl.ds(t * TILE, TILE)], vals.at[t], val_sem.at[t])

    win_copy.start()
    for t in range(tiles):
        val_copy(t).start()
    og_copy.start()

    def clear(w, carry):
        placed[w] = jnp.zeros(placed.shape[1:], placed.dtype)
        return carry

    lax.fori_loop(0, placed.shape[0], clear, 0)
    win_copy.wait()

    def forward(t, carry):
        val_copy(t).wait()
        live = counts[t]
        acc[...] = jnp.zeros_like(acc)
        for span in range(spans):

            @pl.when(span * SPAN < live)
            def _():
                picked = []
                for k in range(SPAN):
                    tile = win[cols[t, span * SPAN + k]]
                    picked.append(jnp.where(span * SPAN + k < live, tile, jnp.zeros_like(tile)))
                acc[...] += jnp.dot(
                    vals[t, :, span * SPAN * TILE:(span + 1) * SPAN * TILE],
                    jnp.concatenate(picked, axis=0), preferred_element_type=jnp.float32)

        agg[pl.ds(pl.multiple_of(t * TILE, TILE), TILE)] = acc[...].astype(agg.dtype)
        return carry

    lax.fori_loop(0, tiles, forward, 0)
    og_copy.wait()
    bias_sum[...] = jnp.zeros_like(bias_sum)

    def dense(t, carry):
        here = pl.ds(pl.multiple_of(t * TILE, TILE), TILE)
        pre_act = jnp.dot(agg[here], weight[...], preferred_element_type=jnp.float32) + bias[...]
        value_part, slope = gelu_parts(pre_act)
        act_out[here] = value_part.astype(act_out.dtype)
        grad = (og[here].astype(jnp.float32) * slope).astype(jnp.bfloat16)
        pre_grad[here] = grad
        bias_sum[...] += jnp.sum(
            grad.astype(jnp.float32).reshape(TILE // 8, 8, grad.shape[1]), axis=0)
        row_grad[t] = lax.dot_general(
            weight[...], grad, (((1,), (1,)), ((), ())), preferred_element_type=jnp.float32
        ).astype(row_grad.dtype)
        return carry

    lax.fori_loop(0, tiles, dense, 0)
    weight_grad = lax.dot_general(
        agg[...], pre_grad[...], (((0,), (0,)), ((), ())), preferred_element_type=jnp.float32
    ) * factor
    bias_grad = jnp.sum(bias_sum[...], axis=0, keepdims=True) * factor
    members, _, cut = grad_out.shape
    in_dim = agg.shape[1]
    for member in range(members):
        columns = slice(member * cut, (member + 1) * cut)
        grad_out[member, :in_dim] = weight_grad[:, columns].astype(grad_out.dtype)
        grad_out[member, in_dim:] = jnp.broadcast_to(
            bias_grad[:, columns], (BIAS_ROWS, cut)).astype(grad_out.dtype)

    def backward(t, carry):
        live = counts[t]
        for span in range(spans):

            @pl.when(span * SPAN < live)
            def _():
                terms = jnp.dot(
                    row_grad[t], vals[t, :, span * SPAN * TILE:(span + 1) * SPAN * TILE],
                    preferred_element_type=jnp.float32)
                for k in range(SPAN):
                    term = terms[:, k * TILE:(k + 1) * TILE]
                    term = jnp.where(span * SPAN + k < live, term, jnp.zeros_like(term))
                    placed[cols[t, span * SPAN + k]] += term

        return carry

    lax.fori_loop(0, tiles, backward, 0)

    def hand_on(w, carry):
        terms_out[w] = placed[w].astype(terms_out.dtype)
        return carry

    lax.fori_loop(0, placed.shape[0], hand_on, 0)


def layer(counts, cols, window, values, weight, bias, out_grad, factor):
    rows, wide = values.shape
    in_dim, out_dim = weight.shape
    tiles = rows // TILE
    window_tiles = SIDES * GROUP * tiles
    dma = pltpu.SemaphoreType.DMA
    window_shape = (window_tiles, TILE, in_dim)
    grad_shape = (GROUP, in_dim + BIAS_ROWS, out_dim // GROUP)
    return pl.pallas_call(
        functools.partial(layer_kernel, factor),
        out_shape=(
            jax.ShapeDtypeStruct((rows, out_dim), jnp.bfloat16),
            jax.ShapeDtypeStruct((window_tiles, in_dim, TILE), jnp.bfloat16),
            jax.ShapeDtypeStruct(grad_shape, jnp.bfloat16),
        ),
        in_specs=[SMEM, SMEM, ANY, ANY, VMEM, VMEM, ANY],
        out_specs=(VMEM, VMEM, VMEM),
        scratch_shapes=[
            pltpu.VMEM((tiles, TILE, wide), jnp.bfloat16),
            pltpu.VMEM(window_shape, jnp.bfloat16),
            pltpu.VMEM((rows, out_dim), jnp.bfloat16),
            pltpu.VMEM((window_tiles, in_dim, TILE), jnp.float32),
            pltpu.VMEM((rows, in_dim), jnp.bfloat16),
            pltpu.VMEM((rows, out_dim), jnp.bfloat16),
            pltpu.VMEM((tiles, in_dim, TILE), jnp.bfloat16),
            pltpu.VMEM((TILE, in_dim), jnp.float32),
            pltpu.VMEM((8, out_dim), jnp.float32),
            dma((tiles,)), dma, dma,
        ],
        compiler_params=pltpu.CompilerParams(vmem_limit_bytes=LIMIT),
        name="layer",
    )(counts, cols, window.reshape(window_shape), values, weight, bias.reshape(1, -1), out_grad)


def reduce_kernel(count, terms, grads, out_ref, whole, near_buf, far_out, far_buf, on_out, on_buf,
                  pair_out, pair_buf, rep_buf, share_out, share_buf, summed, near_send, near_recv,
                  far_send, far_recv, on_send, on_recv, pair_send, pair_recv, rep_send, rep_recv,
                  share_send, share_recv, back_send, back_recv, last_send, last_recv):
    blk, rep = lax.axis_index("blk"), lax.axis_index("rep")
    near, far = partners()
    across = (near + 2) % GROUP
    pair, onward, behind, on_side, pair_side = lines(count)
    sides = (on_side, 1, pair_side)
    step = out_ref.shape[0] // CHUNKS
    f32 = jnp.float32

    barrier = pltpu.get_barrier_semaphore()
    for turn in range(1, GROUP):
        pl.semaphore_signal(
            barrier, inc=1, device_id=(blk, (rep + turn) % GROUP), device_id_type=MESH)
    for turn in range(1, count):
        pl.semaphore_signal(
            barrier, inc=1, device_id=((blk + turn) % count, rep), device_id_type=MESH)
    pl.semaphore_wait(barrier, GROUP + count - 2)

    started = []

    def start(source, target, send, recv, device):
        copy = pltpu.make_async_remote_copy(
            src_ref=source, dst_ref=target, send_sem=send, recv_sem=recv,
            device_id=device, device_id_type=MESH)
        copy.start()
        started.append(copy)
        return copy

    def to_reps(source, target, send, recv):
        return [
            start(source(turn), target(turn), send.at[turn - 1], recv.at[turn - 1],
                  (blk, (rep + turn) % GROUP))
            for turn in range(1, GROUP)
        ]

    def to_blks(source, target, send, recv):
        return [
            start(source(turn), target(turn), send.at[turn - 1], recv.at[turn - 1],
                  ((blk + turn) % count, rep))
            for turn in range(1, count)
        ]

    near_copies, far_copies, on_copies, pair_copies = {}, {}, {}, {}

    def to_near(side, whose):
        near_copies[side, whose] = start(
            terms.at[sides[side], (near, across)[whose]], near_buf.at[side, whose],
            near_send.at[side, whose], near_recv.at[side, whose], (blk, near))

    to_near(0, 1)
    to_near(2, 1)
    rep_copies = to_reps(
        lambda turn: grads.at[(rep + turn) % GROUP], lambda turn: rep_buf.at[turn - 1],
        rep_send, rep_recv)
    for side, whose in ((0, 0), (2, 0), (1, 1), (1, 0)):
        to_near(side, whose)

    def here(chunk):
        return pl.ds(chunk * step, step)

    def chip_sum(side, whose, chunk):
        part = here(chunk)
        return (terms[sides[side], (rep, far)[whose], part].astype(f32)
                + near_buf[side, whose, part].astype(f32))

    def hand(copies, key, value, out, buf, send, recv, device):
        where, part = key[0], here(key[1])
        out[where, part] = value.astype(out.dtype)
        copies[key] = start(
            out.at[where, part], buf.at[where, part], send.at[key[0], key[1]],
            recv.at[key[0], key[1]], device)

    def to_far(side, chunk, value):
        hand(far_copies, (side, chunk), value, far_out, far_buf, far_send, far_recv, (blk, far))

    def to_behind(whose, chunk, value):
        hand(on_copies, (whose, chunk), value, on_out, on_buf, on_send, on_recv, (behind, rep))

    def to_pair(whose, chunk, value):
        hand(pair_copies, (whose, chunk), value, pair_out, pair_buf, pair_send, pair_recv,
             (pair, rep))

    def came(copies, key, buf):
        copies[key].wait_recv()
        return buf[key[0], here(key[1])].astype(f32)

    near_copies[0, 1].wait_recv()
    for over, chunk in zip(TURNED, PLAIN):
        to_behind(1, over, chip_sum(0, 1, over))
        to_far(0, chunk, chip_sum(0, 1, chunk))
    near_copies[2, 1].wait_recv()
    for chunk in PLAIN:
        to_far(2, chunk, chip_sum(2, 1, chunk))

    for copy in rep_copies:
        copy.wait_recv()
    in_dim = grads.shape[1] - BIAS_ROWS
    share = in_dim // count
    total = grads[rep].astype(f32)
    for turn in range(1, GROUP):
        total += rep_buf[turn - 1].astype(f32)
    share_out[:, :share] = total[:in_dim].reshape(count, share, total.shape[1])
    share_out[:, share:] = jnp.broadcast_to(
        total[in_dim:in_dim + SUM_ROWS][None], (count, SUM_ROWS, total.shape[1]))
    share_copies = to_blks(
        lambda turn: share_out.at[(blk + turn) % count], lambda turn: share_buf.at[turn - 1],
        share_send, share_recv)

    near_copies[0, 0].wait_recv()
    for chunk in TURNED:
        to_behind(0, chunk, chip_sum(0, 0, chunk))
    near_copies[1, 1].wait_recv()
    for chunk in PLAIN:
        to_far(1, chunk, chip_sum(1, 1, chunk))
    for chunk in TURNED:
        to_pair(1, chunk, chip_sum(2, 1, chunk) + came(on_copies, (1, chunk), on_buf))
    for chunk in PLAIN:
        to_behind(0, chunk, chip_sum(0, 0, chunk) + came(far_copies, (0, chunk), far_buf))
    near_copies[2, 0].wait_recv()
    for chunk in TURNED:
        to_pair(0, chunk, chip_sum(2, 0, chunk) + came(on_copies, (0, chunk), on_buf))
    for chunk in TURNED:
        to_far(1, chunk, chip_sum(1, 1, chunk) + came(pair_copies, (1, chunk), pair_buf))

    for copy in share_copies:
        copy.wait_recv()
    mine = share_out[blk]
    for turn in range(1, count):
        mine += share_buf[turn - 1]
    summed[blk] = mine
    back_copies = to_blks(
        lambda turn: summed.at[blk], lambda turn: summed.at[blk], back_send, back_recv)

    for chunk in PLAIN:
        to_pair(0, chunk, chip_sum(2, 0, chunk) + came(far_copies, (2, chunk), far_buf)
                + came(on_copies, (0, chunk), on_buf))

    for copy in back_copies:
        copy.wait_recv()
    whole[rep, :in_dim] = summed[:, :share].reshape(in_dim, total.shape[1]).astype(whole.dtype)
    whole[rep, in_dim:] = jnp.broadcast_to(
        summed[0, share:share + 1], (BIAS_ROWS, total.shape[1])).astype(whole.dtype)
    last_copies = to_reps(
        lambda turn: whole.at[rep], lambda turn: whole.at[rep], last_send, last_recv)

    near_copies[1, 0].wait_recv()
    for chunk in TURNED + PLAIN:
        out_ref[here(chunk)] = (
            chip_sum(1, 0, chunk) + came(far_copies, (1, chunk), far_buf)
            + came(pair_copies, (0, chunk), pair_buf))

    for copy in last_copies:
        copy.wait_recv()
    for copy in started:
        copy.wait_send()


def reduce(terms, grads):
    count = lax.axis_size("blk")
    tiles, in_dim, _ = terms.shape
    tiles = tiles // (SIDES * GROUP)
    terms = terms.reshape(SIDES, GROUP, tiles, in_dim, TILE)
    cut = grads.shape[2]
    share = in_dim // count + SUM_ROWS
    piece = (tiles, in_dim, TILE)
    dma = pltpu.SemaphoreType.DMA
    pairs = [(SIDES, 2), (SIDES, CHUNKS), (2, CHUNKS), (2, CHUNKS), (GROUP - 1,), (count - 1,),
             (count - 1,), (GROUP - 1,)]
    return pl.pallas_call(
        functools.partial(reduce_kernel, count),
        out_shape=(
            jax.ShapeDtypeStruct(piece, jnp.float32),
            jax.ShapeDtypeStruct(grads.shape, jnp.bfloat16),
        ),
        in_specs=[VMEM, VMEM],
        out_specs=(VMEM, VMEM),
        scratch_shapes=[
            pltpu.VMEM((SIDES, 2) + piece, jnp.bfloat16),
            pltpu.VMEM((SIDES,) + piece, jnp.bfloat16),
            pltpu.VMEM((SIDES,) + piece, jnp.bfloat16),
            pltpu.VMEM((2,) + piece, jnp.bfloat16),
            pltpu.VMEM((2,) + piece, jnp.bfloat16),
            pltpu.VMEM((2,) + piece, jnp.bfloat16),
            pltpu.VMEM((2,) + piece, jnp.bfloat16),
            pltpu.VMEM((GROUP - 1,) + grads.shape[1:], jnp.bfloat16),
            pltpu.VMEM((count, share, cut), jnp.float32),
            pltpu.VMEM((count - 1, share, cut), jnp.float32),
            pltpu.VMEM((count, share, cut), jnp.float32),
        ] + [dma(shape) for shape in pairs for _ in range(2)],
        compiler_params=pltpu.CompilerParams(
            collective_id=1, has_side_effects=True, vmem_limit_bytes=LIMIT),
        name="reduce_terms",
    )(terms, grads)


def finish_kernel(turned, whole, feature_out, weight_out, bias_out):
    in_dim, cut = weight_out.shape[0], whole.shape[2]
    for tile in range(turned.shape[0]):
        feature_out[tile * TILE:(tile + 1) * TILE] = turned[tile].T
    for member in range(GROUP):
        columns = slice(member * cut, (member + 1) * cut)
        weight_out[:, columns] = whole[member, :in_dim].astype(jnp.float32)
        bias_out[:, columns] = whole[member, in_dim:].astype(jnp.float32)[:1]


def finish(turned, whole):
    tiles, in_dim, _ = turned.shape
    out_dim = GROUP * whole.shape[2]
    return pl.pallas_call(
        finish_kernel,
        out_shape=(
            jax.ShapeDtypeStruct((tiles * TILE, in_dim), jnp.float32),
            jax.ShapeDtypeStruct((in_dim, out_dim), jnp.float32),
            jax.ShapeDtypeStruct((1, out_dim), jnp.float32),
        ),
        in_specs=[VMEM, VMEM],
        out_specs=(VMEM, VMEM, VMEM),
        compiler_params=pltpu.CompilerParams(vmem_limit_bytes=LIMIT),
        name="finish",
    )(turned, whole)


def on_device(features, weight, bias, tile_values, tile_cols, tile_counts, out_grad):
    nodes = features.shape[0] * lax.axis_size("rep") * lax.axis_size("blk")
    window = gather(features)
    activations, terms, grads = layer(
        tile_counts, tile_cols, window, tile_values, weight, bias, out_grad,
        1.0 / math.sqrt(nodes))
    feature_grad, weight_grad, bias_grad = finish(*reduce(terms, grads))
    return activations, feature_grad, weight_grad, bias_grad.reshape(-1)


def solution(mesh):
    assert mesh.shape["rep"] == GROUP
    rows = P(("blk", "rep"), None)
    return jax.shard_map(
        on_device, mesh=mesh,
        in_specs=(rows, P(), P(), rows, rows, P(("blk", "rep")), rows),
        out_specs=(rows, rows, P(), P()), check_vma=False,
    )
```

```python
import functools
import math

import jax
import jax.numpy as jnp
from jax import lax
from jax.experimental import pallas as pl
from jax.experimental.pallas import tpu as pltpu
from jax.sharding import PartitionSpec as P

TILE = 128
SIDES = 3
GROUP = 4
CHUNKS = 4
PLAIN = (0, 1)
TURNED = (2, 3)
DENSE = 2
SPAN = 8
BIAS_ROWS = 16
SUM_ROWS = 8
MESH = pl.DeviceIdType.MESH
VMEM = pl.BlockSpec(memory_space=pltpu.VMEM)
SMEM = pl.BlockSpec(memory_space=pltpu.SMEM)
ANY = pl.BlockSpec(memory_space=pl.ANY)
LIMIT = 56 * 1024 * 1024


def partners():
    rep = lax.axis_index("rep")
    return rep + 1 - 2 * (rep % 2), (rep + 2) % GROUP


def lines(count):
    blk = lax.axis_index("blk")
    odd = blk % 2
    pair = blk + 1 - 2 * odd
    onward = (blk + 2 - 4 * odd + count) % count
    behind = (blk + 4 * odd - 2 + count) % count
    return pair, onward, behind, 2 * odd, 2 - 2 * odd


def gather_kernel(count, own_ref, win_ref, own_sem, pair_send, pair_recv, on_send, on_recv,
                  far_send, far_recv, near_send, near_recv):
    blk, rep = lax.axis_index("blk"), lax.axis_index("rep")
    near, far = partners()
    pair, onward, behind, on_side, pair_side = lines(count)
    sides = (on_side, 1, pair_side)
    rows = own_ref.shape[0] // CHUNKS

    barrier = pltpu.get_barrier_semaphore()
    for device in ((pair, rep), (onward, rep), (behind, rep), (blk, near), (blk, far)):
        pl.semaphore_signal(barrier, inc=1, device_id=device, device_id_type=MESH)
    pl.semaphore_wait(barrier, 5)

    started = []

    def start(side, member, chunk, lands, send, recv, device):
        here = pl.ds(chunk * rows, rows)
        source = win_ref.at[sides[side], (rep, far)[member], here]
        if side == 1 and member == 0:
            source = own_ref.at[here]
        copy = pltpu.make_async_remote_copy(
            src_ref=source, dst_ref=win_ref.at[sides[lands], (rep, far)[member], here],
            send_sem=send, recv_sem=recv, device_id=device, device_id_type=MESH)
        copy.start()
        started.append(copy)
        return copy

    pair_copies, on_copies, far_copies, near_copies = {}, {}, {}, []

    def to_pair(member, chunk):
        pair_copies[member, chunk] = start(
            1, member, chunk, 0, pair_send.at[member, chunk], pair_recv.at[member, chunk],
            (pair, rep))

    def to_onward(member, chunk):
        on_copies[member, chunk] = start(
            2, member, chunk, 0, on_send.at[member, chunk], on_recv.at[member, chunk],
            (onward, rep))

    def to_far(side, chunk):
        far_copies[side, chunk] = start(
            side, 0, chunk, side, far_send.at[side, chunk], far_recv.at[side, chunk], (blk, far))

    def to_near(side, member, chunk):
        near_copies.append(start(
            side, member, chunk, side, near_send.at[side, member, chunk],
            near_recv.at[side, member, chunk], (blk, near)))

    order = PLAIN + TURNED
    for own, over in zip(order, TURNED + PLAIN):
        to_pair(0, own)
        to_far(1, over)
    for chunk in order:
        to_near(1, 0, chunk)
    local = pltpu.make_async_copy(own_ref, win_ref.at[1, rep], own_sem)
    local.start()

    def pair_came(member, chunk):
        pair_copies[member, chunk].wait_recv()
        to_onward(member, chunk)
        if member == 0 and chunk in PLAIN:
            to_far(2, chunk)
        to_near(2, member, chunk)

    def on_came(member, chunk):
        on_copies[member, chunk].wait_recv()
        if member == 0 and chunk in PLAIN:
            to_far(0, chunk)
        to_near(0, member, chunk)

    def far_came(side, chunk):
        far_copies[side, chunk].wait_recv()
        if side == 1 and chunk in TURNED:
            to_pair(1, chunk)
        to_near(side, 1, chunk)

    for own, over in zip(PLAIN, TURNED):
        far_came(1, over)
        pair_came(0, own)
    for chunk in PLAIN:
        on_came(0, chunk)
    for chunk in TURNED:
        pair_came(0, chunk)
    for chunk in PLAIN:
        far_came(1, chunk)
    for chunk in TURNED:
        pair_came(1, chunk)
        on_came(0, chunk)
    for chunk in PLAIN:
        far_came(2, chunk)
        far_came(0, chunk)
    for chunk in TURNED:
        on_came(1, chunk)
    for copy in near_copies:
        copy.wait_recv()
    for copy in started:
        copy.wait_send()
    local.wait()


def gather(features):
    rows, width = features.shape
    dma = pltpu.SemaphoreType.DMA
    return pl.pallas_call(
        functools.partial(gather_kernel, lax.axis_size("blk")),
        out_shape=jax.ShapeDtypeStruct((SIDES, GROUP, rows, width), features.dtype),
        in_specs=[VMEM],
        out_specs=VMEM,
        scratch_shapes=[
            dma, dma((2, CHUNKS)), dma((2, CHUNKS)), dma((2, CHUNKS)), dma((2, CHUNKS)),
            dma((SIDES, CHUNKS)), dma((SIDES, CHUNKS)), dma((SIDES, 2, CHUNKS)),
            dma((SIDES, 2, CHUNKS)),
        ],
        compiler_params=pltpu.CompilerParams(
            collective_id=0, has_side_effects=True, vmem_limit_bytes=LIMIT),
        name="gather_window",
    )(features)


def gelu_parts(pre_act):
    inner = 0.7978845608028654 * (pre_act + 0.044715 * pre_act * pre_act * pre_act)
    tangent = jnp.tanh(inner)
    half = 0.5 * (1.0 + tangent)
    value_part = pre_act * half
    slope = half + 0.5 * pre_act * (
        1.0 - tangent * tangent
    ) * 0.7978845608028654 * (1.0 + 0.134145 * pre_act * pre_act)
    return value_part, slope


def layer_kernel(factor, counts, cols, win_hbm, val_hbm, weight, bias, og_hbm, act_out, terms_out,
                 grad_out, vals, win, og, placed, agg, pre_grad, row_grad, acc, bias_sum, rounded,
                 val_sem, win_sem, og_sem, out_sem):
    tiles, _, wide = vals.shape
    spans = wide // (SPAN * TILE)
    win_copy = pltpu.make_async_copy(win_hbm, win, win_sem)
    og_copy = pltpu.make_async_copy(og_hbm, og, og_sem)

    def val_copy(t):
        return pltpu.make_async_copy(val_hbm.at[pl.ds(t * TILE, TILE)], vals.at[t], val_sem.at[t])

    win_copy.start()
    for t in range(tiles):
        val_copy(t).start()
    og_copy.start()

    def clear(w, carry):
        placed[w] = jnp.zeros(placed.shape[1:], placed.dtype)
        return carry

    lax.fori_loop(0, placed.shape[0], clear, 0)
    win_copy.wait()

    def forward(t, carry):
        val_copy(t).wait()
        live = counts[t]
        acc[...] = jnp.zeros_like(acc)
        for span in range(spans):

            @pl.when(span * SPAN < live)
            def _():
                picked = []
                for k in range(SPAN):
                    tile = win[cols[t, span * SPAN + k]]
                    picked.append(jnp.where(span * SPAN + k < live, tile, jnp.zeros_like(tile)))
                acc[...] += jnp.dot(
                    vals[t, :, span * SPAN * TILE:(span + 1) * SPAN * TILE],
                    jnp.concatenate(picked, axis=0), preferred_element_type=jnp.float32)

        agg[pl.ds(pl.multiple_of(t * TILE, TILE), TILE)] = acc[...].astype(agg.dtype)
        return carry

    lax.fori_loop(0, tiles, forward, 0)
    og_copy.wait()
    bias_sum[...] = jnp.zeros_like(bias_sum)

    taken = DENSE * TILE

    def dense(t, carry):
        here = pl.ds(pl.multiple_of(t * taken, taken), taken)
        pre_act = jnp.dot(agg[here], weight[...], preferred_element_type=jnp.float32) + bias[...]
        value_part, slope = gelu_parts(pre_act)
        act_out[here] = value_part.astype(act_out.dtype)
        grad = (og[here].astype(jnp.float32) * slope).astype(jnp.bfloat16)
        pre_grad[here] = grad
        bias_sum[...] += jnp.sum(
            grad.astype(jnp.float32).reshape(taken // 8, 8, grad.shape[1]), axis=0)
        turned = lax.dot_general(
            weight[...], grad, (((1,), (1,)), ((), ())), preferred_element_type=jnp.float32
        ).astype(row_grad.dtype)
        for k in range(DENSE):
            row_grad[t * DENSE + k] = turned[:, k * TILE:(k + 1) * TILE]
        return carry

    lax.fori_loop(0, tiles // DENSE, dense, 0)
    weight_grad = lax.dot_general(
        agg[...], pre_grad[...], (((0,), (0,)), ((), ())), preferred_element_type=jnp.float32
    ) * factor
    bias_grad = jnp.sum(bias_sum[...], axis=0, keepdims=True) * factor
    members, _, cut = grad_out.shape
    in_dim = agg.shape[1]
    for member in range(members):
        columns = slice(member * cut, (member + 1) * cut)
        grad_out[member, :in_dim] = weight_grad[:, columns].astype(grad_out.dtype)
        grad_out[member, in_dim:] = jnp.broadcast_to(
            bias_grad[:, columns], (BIAS_ROWS, cut)).astype(grad_out.dtype)

    def backward(t, carry):
        live = counts[t]
        for span in range(spans):

            @pl.when(span * SPAN < live)
            def _():
                terms = jnp.dot(
                    row_grad[t], vals[t, :, span * SPAN * TILE:(span + 1) * SPAN * TILE],
                    preferred_element_type=jnp.float32)
                for k in range(SPAN):
                    term = terms[:, k * TILE:(k + 1) * TILE]
                    term = jnp.where(span * SPAN + k < live, term, jnp.zeros_like(term))
                    placed[cols[t, span * SPAN + k]] += term

        return carry

    lax.fori_loop(0, tiles, backward, 0)

    def out_copy(piece):
        here = pl.ds(piece * tiles, tiles)
        return pltpu.make_async_copy(rounded.at[here], terms_out.at[here], out_sem.at[piece])

    pieces = placed.shape[0] // tiles
    for piece in range(pieces):
        here = pl.ds(piece * tiles, tiles)
        rounded[here] = placed[here].astype(rounded.dtype)
        out_copy(piece).start()
    for piece in range(pieces):
        out_copy(piece).wait()


def layer(counts, cols, window, values, weight, bias, out_grad, factor):
    rows, wide = values.shape
    in_dim, out_dim = weight.shape
    tiles = rows // TILE
    window_tiles = SIDES * GROUP * tiles
    dma = pltpu.SemaphoreType.DMA
    window_shape = (window_tiles, TILE, in_dim)
    grad_shape = (GROUP, in_dim + BIAS_ROWS, out_dim // GROUP)
    return pl.pallas_call(
        functools.partial(layer_kernel, factor),
        out_shape=(
            jax.ShapeDtypeStruct((rows, out_dim), jnp.bfloat16),
            jax.ShapeDtypeStruct((window_tiles, in_dim, TILE), jnp.bfloat16),
            jax.ShapeDtypeStruct(grad_shape, jnp.bfloat16),
        ),
        in_specs=[SMEM, SMEM, ANY, ANY, VMEM, VMEM, ANY],
        out_specs=(VMEM, ANY, VMEM),
        scratch_shapes=[
            pltpu.VMEM((tiles, TILE, wide), jnp.bfloat16),
            pltpu.VMEM(window_shape, jnp.bfloat16),
            pltpu.VMEM((rows, out_dim), jnp.bfloat16),
            pltpu.VMEM((window_tiles, in_dim, TILE), jnp.float32),
            pltpu.VMEM((rows, in_dim), jnp.bfloat16),
            pltpu.VMEM((rows, out_dim), jnp.bfloat16),
            pltpu.VMEM((tiles, in_dim, TILE), jnp.bfloat16),
            pltpu.VMEM((TILE, in_dim), jnp.float32),
            pltpu.VMEM((8, out_dim), jnp.float32),
            pltpu.VMEM((window_tiles, in_dim, TILE), jnp.bfloat16),
            dma((tiles,)), dma, dma, dma((SIDES * GROUP,)),
        ],
        compiler_params=pltpu.CompilerParams(vmem_limit_bytes=LIMIT),
        name="layer",
    )(counts, cols, window.reshape(window_shape), values, weight, bias.reshape(1, -1), out_grad)


def reduce_kernel(count, terms, grads, out_ref, whole, near_buf, far_out, far_buf, blk_out,
                  blk_buf, turn_buf, rep_buf, share_out, share_buf, summed, near_send, near_recv,
                  far_send, far_recv, blk_send, blk_recv, turn_send, turn_recv, rep_send, rep_recv,
                  share_send, share_recv, back_send, back_recv, last_send, last_recv):
    blk, rep = lax.axis_index("blk"), lax.axis_index("rep")
    near, far = partners()
    across = (near + 2) % GROUP
    before, after = (blk + count - 1) % count, (blk + 1) % count
    step = out_ref.shape[0] // CHUNKS
    turned = CHUNKS - 1
    plain = range(CHUNKS - 1)
    f32 = jnp.float32

    barrier = pltpu.get_barrier_semaphore()
    for turn in range(1, GROUP):
        pl.semaphore_signal(
            barrier, inc=1, device_id=(blk, (rep + turn) % GROUP), device_id_type=MESH)
    for turn in range(1, count):
        pl.semaphore_signal(
            barrier, inc=1, device_id=((blk + turn) % count, rep), device_id_type=MESH)
    pl.semaphore_wait(barrier, GROUP + count - 2)

    started = []

    def start(source, target, send, recv, device):
        copy = pltpu.make_async_remote_copy(
            src_ref=source, dst_ref=target, send_sem=send, recv_sem=recv,
            device_id=device, device_id_type=MESH)
        copy.start()
        started.append(copy)
        return copy

    def to_reps(source, target, send, recv):
        return [
            start(source(turn), target(turn), send.at[turn - 1], recv.at[turn - 1],
                  (blk, (rep + turn) % GROUP))
            for turn in range(1, GROUP)
        ]

    def to_blks(source, target, send, recv):
        return [
            start(source(turn), target(turn), send.at[turn - 1], recv.at[turn - 1],
                  ((blk + turn) % count, rep))
            for turn in range(1, count)
        ]

    near_copies, far_copies, blk_copies, turn_copies = {}, {}, {}, {}
    ways = ((0, before), (2, after))

    def to_near(side, whose):
        near_copies[side, whose] = start(
            terms.at[side, (near, across)[whose]], near_buf.at[side, whose],
            near_send.at[side, whose], near_recv.at[side, whose], (blk, near))

    to_near(0, 1)
    to_near(2, 1)
    rep_copies = to_reps(
        lambda turn: grads.at[(rep + turn) % GROUP], lambda turn: rep_buf.at[turn - 1],
        rep_send, rep_recv)
    for side, whose in ((0, 0), (2, 0), (1, 1), (1, 0)):
        to_near(side, whose)

    def here(chunk):
        return pl.ds(chunk * step, step)

    def chip_sum(side, whose, chunk):
        part = here(chunk)
        return (terms[side, (rep, far)[whose], part].astype(f32)
                + near_buf[side, whose, part].astype(f32))

    def to_far(side, chunk, value):
        part = here(chunk)
        far_out[side, part] = value.astype(far_out.dtype)
        far_copies[side, chunk] = start(
            far_out.at[side, part], far_buf.at[side, part], far_send.at[side, chunk],
            far_recv.at[side, chunk], (blk, far))

    def to_blk(which, chunk, value):
        part = here(chunk)
        blk_out[which, part] = value.astype(blk_out.dtype)
        blk_copies[which, chunk] = start(
            blk_out.at[which, part], blk_buf.at[which, part], blk_send.at[which, chunk],
            blk_recv.at[which, chunk], (ways[which][1], rep))

    near_copies[0, 1].wait_recv()
    near_copies[2, 1].wait_recv()
    for which, (side, block) in enumerate(ways):
        part = here(turned)
        far_out[side, part] = chip_sum(side, 1, turned).astype(far_out.dtype)
        turn_copies[which] = start(
            far_out.at[side, part], turn_buf.at[which], turn_send.at[which], turn_recv.at[which],
            (block, rep))
    for chunk in plain:
        for side in (0, 2):
            to_far(side, chunk, chip_sum(side, 1, chunk))

    for copy in rep_copies:
        copy.wait_recv()
    in_dim = grads.shape[1] - BIAS_ROWS
    share = in_dim // count
    total = grads[rep].astype(f32)
    for turn in range(1, GROUP):
        total += rep_buf[turn - 1].astype(f32)
    share_out[:, :share] = total[:in_dim].reshape(count, share, total.shape[1])
    share_out[:, share:] = jnp.broadcast_to(
        total[in_dim:in_dim + SUM_ROWS][None], (count, SUM_ROWS, total.shape[1]))
    share_copies = to_blks(
        lambda turn: share_out.at[(blk + turn) % count], lambda turn: share_buf.at[turn - 1],
        share_send, share_recv)

    near_copies[0, 0].wait_recv()
    near_copies[2, 0].wait_recv()
    for which, (side, _) in enumerate(ways):
        to_blk(which, turned, chip_sum(side, 0, turned))
    near_copies[1, 1].wait_recv()
    for chunk in plain:
        to_far(1, chunk, chip_sum(1, 1, chunk))
    own = chip_sum(1, 1, turned)
    for which in range(2):
        turn_copies[which].wait_recv()
        own += turn_buf[which].astype(f32)
    to_far(1, turned, own)

    for chunk in plain:
        for which, (side, _) in enumerate(ways):
            far_copies[side, chunk].wait_recv()
            to_blk(which, chunk,
                   chip_sum(side, 0, chunk) + far_buf[side, here(chunk)].astype(f32))
        if chunk == 0:
            for copy in share_copies:
                copy.wait_recv()
            mine = share_out[blk]
            for turn in range(1, count):
                mine += share_buf[turn - 1]
            summed[blk] = mine
            back_copies = to_blks(
                lambda turn: summed.at[blk], lambda turn: summed.at[blk], back_send, back_recv)

    for copy in back_copies:
        copy.wait_recv()
    whole[rep, :in_dim] = summed[:, :share].reshape(in_dim, total.shape[1]).astype(whole.dtype)
    whole[rep, in_dim:] = jnp.broadcast_to(
        summed[0, share:share + 1], (BIAS_ROWS, total.shape[1])).astype(whole.dtype)
    last_copies = to_reps(
        lambda turn: whole.at[rep], lambda turn: whole.at[rep], last_send, last_recv)

    near_copies[1, 0].wait_recv()
    for chunk in (turned, *plain):
        part = here(chunk)
        for which in range(2):
            blk_copies[which, chunk].wait_recv()
        far_copies[1, chunk].wait_recv()
        total = chip_sum(1, 0, chunk) + far_buf[1, part].astype(f32)
        for which in range(2):
            total += blk_buf[which, part].astype(f32)
        out_ref[part] = total

    for copy in last_copies:
        copy.wait_recv()
    for copy in started:
        copy.wait_send()


def reduce(terms, grads):
    count = lax.axis_size("blk")
    tiles, in_dim, _ = terms.shape
    tiles = tiles // (SIDES * GROUP)
    terms = terms.reshape(SIDES, GROUP, tiles, in_dim, TILE)
    cut = grads.shape[2]
    share = in_dim // count + SUM_ROWS
    piece = (tiles, in_dim, TILE)
    dma = pltpu.SemaphoreType.DMA
    pairs = [(SIDES, 2), (SIDES, CHUNKS), (2, CHUNKS), (2,), (GROUP - 1,), (count - 1,),
             (count - 1,), (GROUP - 1,)]
    return pl.pallas_call(
        functools.partial(reduce_kernel, count),
        out_shape=(
            jax.ShapeDtypeStruct(piece, jnp.float32),
            jax.ShapeDtypeStruct(grads.shape, jnp.bfloat16),
        ),
        in_specs=[VMEM, VMEM],
        out_specs=(VMEM, VMEM),
        scratch_shapes=[
            pltpu.VMEM((SIDES, 2) + piece, jnp.bfloat16),
            pltpu.VMEM((SIDES,) + piece, jnp.bfloat16),
            pltpu.VMEM((SIDES,) + piece, jnp.bfloat16),
            pltpu.VMEM((2,) + piece, jnp.bfloat16),
            pltpu.VMEM((2,) + piece, jnp.bfloat16),
            pltpu.VMEM((2, tiles // CHUNKS) + piece[1:], jnp.bfloat16),
            pltpu.VMEM((GROUP - 1,) + grads.shape[1:], jnp.bfloat16),
            pltpu.VMEM((count, share, cut), jnp.float32),
            pltpu.VMEM((count - 1, share, cut), jnp.float32),
            pltpu.VMEM((count, share, cut), jnp.float32),
        ] + [dma(shape) for shape in pairs for _ in range(2)],
        compiler_params=pltpu.CompilerParams(
            collective_id=1, has_side_effects=True, vmem_limit_bytes=LIMIT),
        name="reduce_terms",
    )(terms, grads)


def finish_kernel(turned, whole, feature_out, weight_out, bias_out):
    in_dim, cut = weight_out.shape[0], whole.shape[2]
    for tile in range(turned.shape[0]):
        feature_out[tile * TILE:(tile + 1) * TILE] = turned[tile].T
    for member in range(GROUP):
        columns = slice(member * cut, (member + 1) * cut)
        weight_out[:, columns] = whole[member, :in_dim].astype(jnp.float32)
        bias_out[:, columns] = whole[member, in_dim:].astype(jnp.float32)[:1]


def finish(turned, whole):
    tiles, in_dim, _ = turned.shape
    out_dim = GROUP * whole.shape[2]
    return pl.pallas_call(
        finish_kernel,
        out_shape=(
            jax.ShapeDtypeStruct((tiles * TILE, in_dim), jnp.float32),
            jax.ShapeDtypeStruct((in_dim, out_dim), jnp.float32),
            jax.ShapeDtypeStruct((1, out_dim), jnp.float32),
        ),
        in_specs=[VMEM, VMEM],
        out_specs=(VMEM, VMEM, VMEM),
        compiler_params=pltpu.CompilerParams(vmem_limit_bytes=LIMIT),
        name="finish",
    )(turned, whole)


def on_device(features, weight, bias, tile_values, tile_cols, tile_counts, out_grad):
    nodes = features.shape[0] * lax.axis_size("rep") * lax.axis_size("blk")
    window = gather(features)
    activations, terms, grads = layer(
        tile_counts, tile_cols, window, tile_values, weight, bias, out_grad,
        1.0 / math.sqrt(nodes))
    feature_grad, weight_grad, bias_grad = finish(*reduce(terms, grads))
    return activations, feature_grad, weight_grad, bias_grad.reshape(-1)


def solution(mesh):
    assert mesh.shape["rep"] == GROUP
    rows = P(("blk", "rep"), None)
    return jax.shard_map(
        on_device, mesh=mesh,
        in_specs=(rows, P(), P(), rows, rows, P(("blk", "rep")), rows),
        out_specs=(rows, rows, P(), P()), check_vma=False,
    )
```
